512 devices in a mesh: row: 32 (over y, x, core), col: 16 (over z).
Axes of the slice: x: 4, y: 4, z: 16, core: 2. Of those that a mesh axis runs over, the one named last changes fastest.
Arguments:
- iterate: float32 [5120, 8192], P('row', 'col'), may hold values from -0.05 to 0.05
Outputs:
- update: float32 [5120, 8192], P('row', 'col')
The draws below stay inside these ranges and needn't reach their ends.
All inputs are finite; a program needn't handle non-finite values.
Results may differ from the reference program's by a relative error of at most 0.0022.
Values may be sent and summed in bfloat16 or wider, within the bound.
A program may use at most 64 MiB of HBM per device.

```python
import math
import jax
import jax.numpy as jnp

ROWS = 5120
COLS = 8192


def draw_iterate(key, part):
    key = jax.random.fold_in(key, 7)
    first = jax.random.fold_in(key, 0)
    base = jnp.clip(jax.random.normal(first, (ROWS, COLS), jnp.float32), -6.0, 6.0)
    values = base * (0.7 / jnp.sqrt(jnp.float32(COLS)))
    values = jnp.clip(values, -0.05, 0.05)
    return values.astype(jnp.float32)


def setup_inputs(seed: int = 0) -> dict:
    arg_keys = jax.random.split(jax.random.key(seed), 2)
    iterate = draw_iterate(jax.random.fold_in(arg_keys[1], 71), 0)
    return {"iterate": iterate}


coef_a = 3.4445
coef_b = -4.775
coef_c = 2.0315

def reference(iterate):
    iter_b = iterate.astype(jnp.bfloat16)
    gram = jnp.dot(iter_b, iter_b.T, preferred_element_type=jnp.float32)
    gram_b = gram.astype(jnp.bfloat16)
    square = jnp.dot(gram_b, gram_b, preferred_element_type=jnp.float32)
    mixed = (coef_b * gram + coef_c * square).astype(jnp.bfloat16)
    result = coef_a * iterate + jnp.dot(mixed, iter_b, preferred_element_type=jnp.float32)
    return 0.2 * math.sqrt(COLS) * result
```

```python
import functools
import math

import jax
import jax.numpy as jnp
from jax import lax
from jax.experimental import pallas as pl
from jax.experimental.pallas import tpu as pltpu
from jax.sharding import PartitionSpec as P

coef_a = 3.4445
coef_b = -4.775
coef_c = 2.0315

NX = 4
NY = 4
NZ = 16
BLOCK = 160
HALF = 80
WIDE = 640
COLS = 512
SUBS = 2
MESH = pl.DeviceIdType.MESH


class Copies:
    def __init__(self):
        self.started = []

    def start(self, src, dst, send_sem, recv_sem, device):
        copy = pltpu.make_async_remote_copy(
            src_ref=src,
            dst_ref=dst,
            send_sem=send_sem,
            recv_sem=recv_sem,
            device_id=device,
            device_id_type=MESH,
        )
        copy.start()
        self.started.append(copy)

    def finish(self):
        for copy in self.started:
            copy.wait_send()


def arrived(ref, send_sem, recv_sem, device):
    pltpu.make_async_remote_copy(
        src_ref=ref,
        dst_ref=ref,
        send_sem=send_sem,
        recv_sem=recv_sem,
        device_id=device,
        device_id_type=MESH,
    ).wait_recv()


class PlaneGather:
    def __init__(self, copies, way, place, view, cut, total, send, recv):
        self.copies, self.way, self.place, self.view = copies, way, place, view
        self.cuts = ((0, cut), (cut, total - cut))
        self.send, self.recv = send, recv

    def coords(self, a, b):
        x, y, _, _ = self.place
        dx, dy = (a, b) if self.way == 0 else (b, a)
        return lax.rem(x + (dx % 4), 4), lax.rem(y + (dy % 4), 4)

    def block(self, a, b, core=None):
        x, y = self.coords(a, b)
        core = self.place[2] if core is None else core
        return core * 16 + y * 4 + x

    def device(self, a, b):
        x, y = self.coords(a, b)
        return {"row": (y * 4 + x) * 2 + self.place[2], "col": self.place[3]}

    def sibling(self):
        x, y, core, z = self.place
        return {"row": (y * 4 + x) * 2 + 1 - core, "col": z}

    def half(self, index, part):
        start, size = self.cuts[part]
        return self.view(index).at[pl.ds(start, size), :]

    def push(self, a, b, to, slot, part=None):
        index = self.block(a, b)
        ref = self.view(index) if part is None else self.half(index, part)
        device = self.sibling() if to is None else self.device(*to)
        self.copies.start(ref, ref, self.send.at[slot], self.recv.at[slot], device)

    def wait(self, a, b, slot, part=None, core=None):
        index = self.block(a, b, core)
        ref = self.view(index) if part is None else self.half(index, part)
        arrived(ref, self.send.at[slot], self.recv.at[slot], self.sibling())

    def second(self, a):
        k = a % 4
        self.push(a, 0, (0, 1), 4 + 2 * k)
        self.push(a, 0, (0, -1), 5 + 2 * k)

    def other(self, a, b):
        self.push(a, b, None, 20 + (a % 4) * 4 + b % 4)

    def own(self):
        self.push(0, 0, (1, 0), 0)
        self.push(0, 0, (-1, 0), 1)
        self.second(0)
        self.other(0, 0)

    def first(self):
        self.wait(-1, 0, 0)
        self.push(-1, 0, (1, 0), 2, part=0)
        self.second(-1)
        self.wait(1, 0, 1)
        self.push(1, 0, (-1, 0), 3, part=1)
        self.second(1)
        self.other(-1, 0)
        self.other(1, 0)

    def first_far(self):
        self.wait(2, 0, 2, part=0)
        self.wait(2, 0, 3, part=1)
        self.second(2)
        self.other(2, 0)

    def then(self, a):
        k = a % 4
        self.wait(a, -1, 4 + 2 * k)
        self.push(a, -1, (0, 1), 12 + 2 * k, part=0)
        self.wait(a, 1, 5 + 2 * k)
        self.push(a, 1, (0, -1), 13 + 2 * k, part=1)
        self.other(a, -1)
        self.other(a, 1)

    def then_far(self, a):
        k = a % 4
        self.wait(a, 2, 12 + 2 * k, part=0)
        self.wait(a, 2, 13 + 2 * k, part=1)
        self.other(a, 2)

    def others(self):
        for a in range(4):
            for b in range(4):
                self.wait(a, b, 20 + a * 4 + b, core=1 - self.place[2])


class RingGather:
    def __init__(self, copies, buf, place, up, down, send, recv):
        self.copies, self.buf, self.z = copies, buf, place[3]
        self.up, self.down, self.send, self.recv = up, down, send, recv

    def plane(self, d):
        return lax.rem(self.z + d % NZ, NZ)

    def step(self, s):
        if s > 1:
            self.wait_up(s - 1)
        ref = self.buf.at[self.plane(1 - s)]
        self.copies.start(ref, ref, self.send.at[0, s], self.recv.at[0, s], self.up)
        if s <= 7:
            if s > 1:
                self.wait_down(s - 1)
            ref = self.buf.at[self.plane(s - 1)]
            self.copies.start(ref, ref, self.send.at[1, s], self.recv.at[1, s], self.down)

    def wait_up(self, s):
        arrived(self.buf.at[self.plane(-s)], self.send.at[0, s], self.recv.at[0, s], self.up)

    def wait_down(self, s):
        arrived(self.buf.at[self.plane(s)], self.send.at[1, s], self.recv.at[1, s], self.down)


def kernel(
    x_ref, out_ref,
    slab, cw, ccw, gram, grow, gcol, mrow,
    xs, xr, rs_s, rs_r, gs, gr, cs, cr, ms, mr,
):
    row, z = lax.axis_index("row"), lax.axis_index("col")
    core = lax.rem(row, 2)
    x = lax.rem(row // 2, 4)
    y = row // 8
    zh, zl = z // 2, lax.rem(z, 2)
    place = (x, y, core, z)
    me = core * 16 + y * 4 + x
    up = {"row": row, "col": lax.rem(z + 1, NZ)}
    down = {"row": row, "col": lax.rem(z + NZ - 1, NZ)}

    copies = Copies()
    gather_x = [
        PlaneGather(
            copies, w, place, lambda i, w=w: slab.at[w, i], 80, BLOCK, xs.at[w], xr.at[w]
        )
        for w in range(2)
    ]

    barrier = pltpu.get_barrier_semaphore()
    g0 = gather_x[0]
    for device in (
        g0.device(1, 0), g0.device(-1, 0), g0.device(0, 1), g0.device(0, -1), g0.sibling(), up, down,
    ):
        pl.semaphore_signal(barrier, inc=1, device_id=device, device_id_type=MESH)
    slab[0, me] = x_ref[:, 0:256].astype(jnp.bfloat16)
    slab[1, me] = x_ref[:, 256:512].astype(jnp.bfloat16)
    pl.semaphore_wait(barrier, 7)

    for g in gather_x:
        g.own()
    for g in gather_x:
        g.first()
    for g in gather_x:
        g.first_far()
    for a in (0, -1, 1, 2):
        for g in gather_x:
            g.then(a)
    for a in (0, -1, 1, 2):
        for g in gather_x:
            g.then_far(a)
    for g in gather_x:
        g.others()

    def share(d):
        dh, dl = d // 2, lax.rem(d, 2)
        value = None
        for h in range(2):
            left = slab[h, me, pl.ds(pl.multiple_of(dl * HALF, 16), HALF), :]
            right = slab[h, pl.ds(dh * 4, 4)].reshape(WIDE, 256)
            term = lax.dot_general(
                left, right, (((1,), (1,)), ((), ())), preferred_element_type=jnp.float32
            )
            value = term if value is None else value + term
        return value

    rows = HALF // SUBS

    def piece(buf, slot, j):
        return buf.at[slot, pl.ds(j * rows, rows), :]

    def ring_copy(way, buf, slot, j, device):
        return pltpu.make_async_remote_copy(
            src_ref=piece(buf, slot, j),
            dst_ref=piece(buf, slot + 1, j),
            send_sem=rs_s.at[way, slot, j],
            recv_sem=rs_r.at[way, slot + 1, j],
            device_id=device,
            device_id_type=MESH,
        )

    def ring_arrived(way, buf, slot, j):
        arrived(piece(buf, slot, j), rs_s.at[way, slot, j], rs_r.at[way, slot, j], up)

    def ring_step(ways, slot):
        for way in ways:
            buf, device = (cw, up) if way == 0 else (ccw, down)
            d = lax.rem(z + 8 - slot, NZ) if way == 0 else lax.rem(z + 9 + slot, NZ)
            part = share(d)
            for j in range(SUBS):
                ring_arrived(way, buf, slot, j)
                buf[slot, j * rows : (j + 1) * rows, :] += part[j * rows : (j + 1) * rows]
                ring_copy(way, buf, slot, j, device).start()

    for way, buf, device, d in ((0, cw, up, z + 8), (1, ccw, down, z + 9)):
        buf[0] = share(lax.rem(d, NZ))
        for j in range(SUBS):
            ring_copy(way, buf, 0, j, device).start()

    @pl.loop(1, 7)
    def _(slot):
        ring_step((0, 1), slot)

    ring_step((0,), 7)
    gram[...] = share(z)
    for j in range(SUBS):
        ring_arrived(1, ccw, 7, j)
        ring_arrived(0, cw, 8, j)
    gram[...] += cw[8] + ccw[7]

    gather_g = RingGather(copies, grow, place, up, down, gs, gr)
    gather_c = [
        PlaneGather(
            copies, w, place, lambda i, half=half: gcol.at[i, half], 48, HALF, cs.at[w], cr.at[w]
        )
        for w, half in ((0, zl), (1, 1 - zl))
    ]
    gb = gram[...].astype(jnp.bfloat16)
    grow[z] = gb
    gcol[me, zl] = gb
    gather_g.step(1)
    gather_c[0].own()
    gather_g.step(2)

    mate = jnp.where(zl == 0, 1, NZ - 1)
    gcol[me, 1 - zl] = grow[lax.rem(z + mate, NZ)]
    gather_c[1].own()
    gather_c[0].first()
    gather_g.step(3)
    gather_c[1].first()
    gather_c[0].first_far()
    gather_c[1].first_far()
    gather_g.step(4)
    for i, a in enumerate((0, -1, 1, 2)):
        for g in gather_c:
            g.then(a)
        gather_g.step(5 + i)
    for a in (0, -1, 1, 2):
        for g in gather_c:
            g.then_far(a)
    for g in gather_c:
        g.others()
    gather_g.wait_up(8)
    gather_g.wait_down(7)

    def square_step(i, total):
        return total + jnp.dot(
            grow[2 * i + zl],
            gcol[pl.ds(4 * i, 4)].reshape(WIDE, WIDE),
            preferred_element_type=jnp.float32,
        )

    square = lax.fori_loop(0, 8, square_step, jnp.zeros((HALF, WIDE), jnp.float32))
    mrow[z] = (coef_b * gram[...] + coef_c * square).astype(jnp.bfloat16)

    gather_m = RingGather(copies, mrow, place, up, down, ms, mr)
    for s in range(1, 9):
        gather_m.step(s)
    gather_m.wait_up(8)
    gather_m.wait_down(7)

    scale = 0.2 * math.sqrt(COLS * NZ)
    out_ref[...] = coef_a * x_ref[...]

    @pl.loop(0, 8)
    def _(i):
        left = mrow[pl.ds(2 * i, 2)].reshape(BLOCK, WIDE)
        for h in range(2):
            right = slab[h, pl.ds(4 * i, 4)].reshape(WIDE, 256)
            out_ref[:, h * 256 : (h + 1) * 256] += jnp.dot(
                left, right, preferred_element_type=jnp.float32
            )

    out_ref[...] = scale * out_ref[...]

    copies.finish()

    for j in range(SUBS):

        @pl.loop(0, 7)
        def _(slot):
            ring_copy(0, cw, slot, j, up).wait_send()
            ring_copy(1, ccw, slot, j, down).wait_send()

        ring_copy(0, cw, 7, j, up).wait_send()


def local(iterate):
    dma = pltpu.SemaphoreType.DMA
    return pl.pallas_call(
        kernel,
        out_shape=jax.ShapeDtypeStruct((BLOCK, COLS), jnp.float32),
        in_specs=[pl.BlockSpec(memory_space=pltpu.VMEM)],
        out_specs=pl.BlockSpec(memory_space=pltpu.VMEM),
        scratch_shapes=[
            pltpu.VMEM((2, 32, BLOCK, 256), jnp.bfloat16),
            pltpu.VMEM((9, HALF, WIDE), jnp.float32),
            pltpu.VMEM((8, HALF, WIDE), jnp.float32),
            pltpu.VMEM((HALF, WIDE), jnp.float32),
            pltpu.VMEM((NZ, HALF, WIDE), jnp.bfloat16),
            pltpu.VMEM((32, 2, HALF, WIDE), jnp.bfloat16),
            pltpu.VMEM((NZ, HALF, WIDE), jnp.bfloat16),
            dma((2, 36)),
            dma((2, 36)),
            dma((2, 9, SUBS)),
            dma((2, 9, SUBS)),
            dma((2, 9)),
            dma((2, 9)),
            dma((2, 36)),
            dma((2, 36)),
            dma((2, 9)),
            dma((2, 9)),
        ],
        compiler_params=pltpu.CompilerParams(
            collective_id=0, has_side_effects=True, vmem_limit_bytes=48 * 1024 * 1024
        ),
        cost_estimate=pl.CostEstimate(
            flops=2300000000, bytes_accessed=700000, transcendentals=0
        ),
    )(iterate)


def solution(mesh):
    return jax.shard_map(
        local,
        mesh=mesh,
        in_specs=(P("row", "col"),),
        out_specs=P("row", "col"),
        check_vma=False,
    )
```

```python
import functools
import math

import jax
import jax.numpy as jnp
from jax import lax
from jax.experimental import pallas as pl
from jax.experimental.pallas import tpu as pltpu
from jax.sharding import PartitionSpec as P

coef_a = 3.4445
coef_b = -4.775
coef_c = 2.0315

NX = 4
NY = 4
NZ = 16
BLOCK = 160
HALF = 80
WIDE = 640
COLS = 512
SUBS = 2
PIECES = 5
MESH = pl.DeviceIdType.MESH


def remote(ref, send_sem, recv_sem, device):
    return pltpu.make_async_remote_copy(
        src_ref=ref,
        dst_ref=ref,
        send_sem=send_sem,
        recv_sem=recv_sem,
        device_id=device,
        device_id_type=MESH,
    )


class PlaneGather:
    def __init__(self, way, place, view, cut, total, send, recv):
        self.way, self.place, self.view = way, place, view
        self.cuts = ((0, cut), (cut, total - cut))
        self.send, self.recv = send, recv

    def coords(self, a, b):
        x, y, _, _ = self.place
        dx, dy = (a, b) if self.way == 0 else (b, a)
        return lax.rem(x + (dx % 4), 4), lax.rem(y + (dy % 4), 4)

    def block(self, a, b, core=None):
        x, y = self.coords(a, b)
        core = self.place[2] if core is None else core
        return core * 16 + y * 4 + x

    def device(self, a, b):
        x, y = self.coords(a, b)
        return {"row": (y * 4 + x) * 2 + self.place[2], "col": self.place[3]}

    def sibling(self):
        x, y, core, z = self.place
        return {"row": (y * 4 + x) * 2 + 1 - core, "col": z}

    def half(self, index, part):
        start, size = self.cuts[part]
        return self.view(index).at[pl.ds(start, size), :]

    def push(self, a, b, to, slot, part=None):
        index = self.block(a, b)
        ref = self.view(index) if part is None else self.half(index, part)
        device = self.sibling() if to is None else self.device(*to)
        remote(ref, self.send, self.recv.at[slot], device).start()

    def wait(self, a, b, slot, part=None, core=None):
        index = self.block(a, b, core)
        ref = self.view(index) if part is None else self.half(index, part)
        remote(ref, self.send, self.recv.at[slot], self.sibling()).wait_recv()

    def second(self, a):
        k = a % 4
        self.push(a, 0, (0, 1), 4 + 2 * k)
        self.push(a, 0, (0, -1), 5 + 2 * k)

    def other(self, a, b):
        self.push(a, b, None, 20)

    def own(self):
        self.push(0, 0, (1, 0), 0)
        self.push(0, 0, (-1, 0), 1)
        self.second(0)
        self.other(0, 0)

    def first(self):
        self.wait(-1, 0, 0)
        self.push(-1, 0, (1, 0), 2, part=0)
        self.second(-1)
        self.wait(1, 0, 1)
        self.push(1, 0, (-1, 0), 3, part=1)
        self.second(1)
        self.other(-1, 0)
        self.other(1, 0)

    def first_far(self):
        self.wait(2, 0, 2, part=0)
        self.wait(2, 0, 3, part=1)
        self.second(2)
        self.other(2, 0)

    def then(self, a):
        k = a % 4
        self.wait(a, -1, 4 + 2 * k)
        self.push(a, -1, (0, 1), 12 + 2 * k, part=0)
        self.wait(a, 1, 5 + 2 * k)
        self.push(a, 1, (0, -1), 13 + 2 * k, part=1)
        self.other(a, -1)
        self.other(a, 1)

    def then_far(self, a):
        k = a % 4
        self.wait(a, 2, 12 + 2 * k, part=0)
        self.wait(a, 2, 13 + 2 * k, part=1)
        self.other(a, 2)

    def others(self, blocks):
        remote(blocks, self.send, self.recv.at[20], self.sibling()).wait_recv()


class RingGather:
    def __init__(self, buf, place, stride, send, recv):
        self.buf, self.stride, self.send, self.recv = buf, stride, send, recv
        self.row, self.z = (place[1] * 4 + place[0]) * 2 + place[2], place[3]
        self.far = NZ // stride // 2

    def plane(self, d):
        return lax.rem(self.z + d * self.stride + 2 * NZ, NZ)

    def copy(self, way, s, j):
        ref = self.buf.at[self.plane(1 - s if way == 0 else s - 1) // self.stride, pl.ds(j * 16, 16), :]
        device = {"row": self.row, "col": self.plane(1 if way == 0 else -1)}
        return remote(ref, self.send, self.recv.at[way, s, j], device)

    def wait(self, way, s, j):
        ref = self.buf.at[self.plane(-s if way == 0 else s) // self.stride, pl.ds(j * 16, 16), :]
        device = {"row": self.row, "col": self.plane(1)}
        remote(ref, self.send, self.recv.at[way, s, j], device).wait_recv()

    def pieces(self, last):
        for j in range(PIECES):
            for way in range(2):
                if not last or (way == 0) == (j < 3):
                    yield way, j

    def step(self, s, first=False, last=False):
        for way, j in self.pieces(last):
            if not first:
                self.wait(way, s - 1, j)
            self.copy(way, s, j).start()
        if last:
            for way, j in self.pieces(False):
                if (way == 0) != (j < 3):
                    self.wait(way, s - 1, j)

    def end(self):
        for way, j in self.pieces(True):
            self.wait(way, self.far, j)


def kernel(
    x_ref, out_ref,
    slab, cw, ccw, gram, grow, gcol, mrow,
    sent, xr, rs_r, gr, cr, mr,
):
    row, z = lax.axis_index("row"), lax.axis_index("col")
    core = lax.rem(row, 2)
    x = lax.rem(row // 2, 4)
    y = row // 8
    zh, zl = z // 2, lax.rem(z, 2)
    place = (x, y, core, z)
    me = core * 16 + y * 4 + x
    up = {"row": row, "col": lax.rem(z + 1, NZ)}
    down = {"row": row, "col": lax.rem(z + NZ - 1, NZ)}

    gather_x = [
        PlaneGather(
            w, place, lambda i, w=w: slab.at[w, i], 80, BLOCK, sent.at[0], xr.at[w]
        )
        for w in range(2)
    ]

    barrier = pltpu.get_barrier_semaphore()
    g0 = gather_x[0]
    for device in (
        g0.device(1, 0), g0.device(-1, 0), g0.device(0, 1), g0.device(0, -1), g0.sibling(), up, down,
    ):
        pl.semaphore_signal(barrier, inc=1, device_id=device, device_id_type=MESH)
    slab[0, me] = x_ref[:, 0:256].astype(jnp.bfloat16)
    slab[1, me] = x_ref[:, 256:512].astype(jnp.bfloat16)
    pl.semaphore_wait(barrier, 7)

    for g in gather_x:
        g.own()
    for g in gather_x:
        g.first()
    for g in gather_x:
        g.then(0)
    for g in gather_x:
        g.first_far()
    for a in (-1, 1, 2):
        for g in gather_x:
            g.then(a)
    for a in (0, -1, 1, 2):
        for g in gather_x:
            g.then_far(a)
    theirs = pl.ds((1 - core) * 16, 16)
    for g in gather_x:
        g.others(slab.at[g.way, theirs])

    def share(d):
        dh, dl = d // 2, lax.rem(d, 2)
        value = None
        for h in range(2):
            left = slab[h, me, pl.ds(pl.multiple_of(dl * HALF, 16), HALF), :]
            right = slab[h, pl.ds(dh * 4, 4)].reshape(WIDE, 256)
            term = lax.dot_general(
                left, right, (((1,), (1,)), ((), ())), preferred_element_type=jnp.float32
            )
            value = term if value is None else value + term
        return value

    rows = HALF // SUBS

    def piece(buf, slot, j):
        return buf.at[slot, pl.ds(j * rows, rows), :]

    def ring_copy(way, buf, slot, j, device):
        return pltpu.make_async_remote_copy(
            src_ref=piece(buf, slot, j),
            dst_ref=piece(buf, slot + 1, j),
            send_sem=sent.at[1 + way],
            recv_sem=rs_r.at[way, slot + 1, j],
            device_id=device,
            device_id_type=MESH,
        )

    def ring_arrived(way, buf, slot, j):
        remote(piece(buf, slot, j), sent.at[1 + way], rs_r.at[way, slot, j], up).wait_recv()

    def ring_step(ways, slot):
        for way in ways:
            buf, device = (cw, up) if way == 0 else (ccw, down)
            d = lax.rem(z + 8 - slot, NZ) if way == 0 else lax.rem(z + 9 + slot, NZ)
            part = share(d)
            for j in range(SUBS):
                ring_arrived(way, buf, slot, j)
                buf[slot, j * rows : (j + 1) * rows, :] += part[j * rows : (j + 1) * rows]
                ring_copy(way, buf, slot, j, device).start()

    for way, buf, device, d in ((0, cw, up, z + 8), (1, ccw, down, z + 9)):
        buf[0] = share(lax.rem(d, NZ))
        for j in range(SUBS):
            ring_copy(way, buf, 0, j, device).start()

    @pl.loop(1, 7)
    def _(slot):
        ring_step((0, 1), slot)

    ring_step((0,), 7)
    gram[...] = share(z)
    for j in range(SUBS):
        ring_arrived(1, ccw, 7, j)
        ring_arrived(0, cw, 8, j)
    gram[...] += cw[8] + ccw[7]

    gather_g = RingGather(grow, place, 2, sent.at[4], gr)
    gather_c = [
        PlaneGather(
            w, place, lambda i, half=half: gcol.at[i, half], 48, HALF, sent.at[3], cr.at[w]
        )
        for w, half in ((0, zl), (1, 1 - zl))
    ]
    gb = gram[...].astype(jnp.bfloat16)
    gcol[me, zl] = gb
    grow[zh] = gb
    mate = {"row": row, "col": z + 1 - 2 * zl}
    remote(gcol.at[me, zl], sent.at[6], cr.at[0, 21], mate).start()
    gather_c[0].own()
    gather_g.step(1, first=True)
    remote(gcol.at[me, 1 - zl], sent.at[3], cr.at[0, 21], mate).wait_recv()
    gather_c[1].own()
    gather_c[0].first()
    gather_c[0].then(0)
    gather_g.step(2)
    gather_c[1].first()
    gather_c[1].then(0)
    gather_c[0].first_far()
    gather_g.step(3)
    gather_c[0].then(-1)
    gather_c[0].then(1)
    gather_c[1].first_far()
    gather_c[1].then(-1)
    gather_g.step(4, last=True)
    gather_c[1].then(1)
    for g in gather_c:
        g.then(2)
    for a in (0, -1, 1, 2):
        for g in gather_c:
            g.then_far(a)
    gather_c[0].others(gcol.at[theirs, zl])
    gather_c[1].others(gcol.at[theirs, 1 - zl])
    gather_g.end()

    def square_step(i, total):
        return total + jnp.dot(
            grow[i],
            gcol[pl.ds(4 * i, 4)].reshape(WIDE, WIDE),
            preferred_element_type=jnp.float32,
        )

    square = lax.fori_loop(0, 8, square_step, jnp.zeros((HALF, WIDE), jnp.float32))
    mrow[z] = (coef_b * gram[...] + coef_c * square).astype(jnp.bfloat16)

    def product(d):
        q = lax.rem(z + d + NZ, NZ)
        rows_q = pl.ds(pl.multiple_of(lax.rem(q, 2) * HALF, 16), HALF)
        for h in range(2):
            right = slab[h, pl.ds(q // 2 * 4, 4)].reshape(WIDE, 256)
            out_ref[rows_q, h * 256 : (h + 1) * 256] += jnp.dot(
                mrow[q], right, preferred_element_type=jnp.float32
            )

    gather_m = RingGather(mrow, place, 1, sent.at[5], mr)
    gather_m.step(1, first=True)
    out_ref[...] = coef_a * x_ref[...]
    product(0)

    @pl.loop(2, 8)
    def _(s):
        gather_m.step(s)
        product(1 - s)
        product(s - 1)

    gather_m.step(8, last=True)
    product(-7)
    product(7)
    gather_m.end()
    product(8)
    out_ref[...] = (0.2 * math.sqrt(COLS * NZ)) * out_ref[...]

    for k, ref in (
        (0, slab.at[:, pl.ds(0, 31)]),
        (1, cw.at[pl.ds(0, 8)]),
        (2, ccw.at[pl.ds(0, 7)]),
        (3, gcol.at[pl.ds(0, 31)]),
        (6, gcol.at[31, 0]),
        (4, grow.at[pl.ds(0, 7)]),
        (5, mrow.at[pl.ds(0, 15)]),
    ):
        remote(ref, sent.at[k], sent.at[k], up).wait_send()


def local(iterate):
    dma = pltpu.SemaphoreType.DMA
    return pl.pallas_call(
        kernel,
        out_shape=jax.ShapeDtypeStruct((BLOCK, COLS), jnp.float32),
        in_specs=[pl.BlockSpec(memory_space=pltpu.VMEM)],
        out_specs=pl.BlockSpec(memory_space=pltpu.VMEM),
        scratch_shapes=[
            pltpu.VMEM((2, 32, BLOCK, 256), jnp.bfloat16),
            pltpu.VMEM((9, HALF, WIDE), jnp.float32),
            pltpu.VMEM((8, HALF, WIDE), jnp.float32),
            pltpu.VMEM((HALF, WIDE), jnp.float32),
            pltpu.VMEM((NZ // 2, HALF, WIDE), jnp.bfloat16),
            pltpu.VMEM((32, 2, HALF, WIDE), jnp.bfloat16),
            pltpu.VMEM((NZ, HALF, WIDE), jnp.bfloat16),
            dma((7,)),
            dma((2, 21)),
            dma((2, 9, SUBS)),
            dma((2, 5, PIECES)),
            dma((2, 22)),
            dma((2, 9, PIECES)),
        ],
        compiler_params=pltpu.CompilerParams(
            collective_id=0, has_side_effects=True, vmem_limit_bytes=48 * 1024 * 1024
        ),
        cost_estimate=pl.CostEstimate(
            flops=2300000000, bytes_accessed=700000, transcendentals=0
        ),
    )(iterate)


def solution(mesh):
    return jax.shard_map(
        local,
        mesh=mesh,
        in_specs=(P("row", "col"),),
        out_specs=P("row", "col"),
        check_vma=False,
    )
```

```python
import functools
import math

import jax
import jax.numpy as jnp
from jax import lax
from jax.experimental import pallas as pl
from jax.experimental.pallas import tpu as pltpu
from jax.sharding import PartitionSpec as P

coef_a = 3.4445
coef_b = -4.775
coef_c = 2.0315

NX = 4
NY = 4
NZ = 16
BLOCK = 160
HALF = 80
WIDE = 320
COLS = 512
CUT = 48
STRAIGHT = 8
LONG = 2 * (8 - STRAIGHT) + 1
PIECES = 5
MESH = pl.DeviceIdType.MESH


def remote(ref, send_sem, recv_sem, device):
    return pltpu.make_async_remote_copy(
        src_ref=ref,
        dst_ref=ref,
        send_sem=send_sem,
        recv_sem=recv_sem,
        device_id=device,
        device_id_type=MESH,
    )


class PlaneGather:
    def __init__(self, way, place, view, cut, total, send, recv):
        self.way, self.place, self.view = way, place, view
        self.cuts = ((0, cut), (cut, total - cut))
        self.send, self.recv = send, recv

    def coords(self, a, b):
        x, y, _, _ = self.place
        dx, dy = (a, b) if self.way == 0 else (b, a)
        return lax.rem(x + (dx % 4), 4), lax.rem(y + (dy % 4), 4)

    def block(self, a, b, core=None):
        x, y = self.coords(a, b)
        core = self.place[2] if core is None else core
        return core * 16 + y * 4 + x

    def device(self, a, b):
        x, y = self.coords(a, b)
        return {"row": (y * 4 + x) * 2 + self.place[2], "col": self.place[3]}

    def sibling(self):
        x, y, core, z = self.place
        return {"row": (y * 4 + x) * 2 + 1 - core, "col": z}

    def half(self, index, part):
        start, size = self.cuts[part]
        return self.view(index).at[pl.ds(start, size), :]

    def push(self, a, b, to, slot, part=None):
        index = self.block(a, b)
        ref = self.view(index) if part is None else self.half(index, part)
        device = self.sibling() if to is None else self.device(*to)
        remote(ref, self.send, self.recv.at[slot], device).start()

    def wait(self, a, b, slot, part=None, core=None):
        index = self.block(a, b, core)
        ref = self.view(index) if part is None else self.half(index, part)
        remote(ref, self.send, self.recv.at[slot], self.sibling()).wait_recv()

    def second(self, a):
        k = a % 4
        self.push(a, 0, (0, 1), 4 + 2 * k)
        self.push(a, 0, (0, -1), 5 + 2 * k)

    def other(self, a, b):
        self.push(a, b, None, 20)

    def own(self):
        self.push(0, 0, (1, 0), 0)
        self.push(0, 0, (-1, 0), 1)
        self.second(0)
        self.other(0, 0)

    def first(self):
        self.wait(-1, 0, 0)
        self.push(-1, 0, (1, 0), 2, part=0)
        self.second(-1)
        self.wait(1, 0, 1)
        self.push(1, 0, (-1, 0), 3, part=1)
        self.second(1)
        self.other(-1, 0)
        self.other(1, 0)

    def first_far(self):
        self.wait(2, 0, 2, part=0)
        self.wait(2, 0, 3, part=1)
        self.second(2)
        self.other(2, 0)

    def then(self, a):
        k = a % 4
        self.wait(a, -1, 4 + 2 * k)
        self.push(a, -1, (0, 1), 12 + 2 * k, part=0)
        self.wait(a, 1, 5 + 2 * k)
        self.push(a, 1, (0, -1), 13 + 2 * k, part=1)
        self.other(a, -1)
        self.other(a, 1)

    def then_far(self, a):
        k = a % 4
        self.wait(a, 2, 12 + 2 * k, part=0)
        self.wait(a, 2, 13 + 2 * k, part=1)
        self.other(a, 2)

    def others(self, blocks):
        remote(blocks, self.send, self.recv.at[20], self.sibling()).wait_recv()


STAGES = (
    lambda g: g.own(),
    lambda g: g.first(),
    lambda g: g.then(0),
    lambda g: g.first_far(),
    lambda g: g.then(-1),
    lambda g: g.then(1),
    lambda g: g.then_far(0),
    lambda g: g.then(2),
    lambda g: g.then_far(-1),
    lambda g: g.then_far(1),
    lambda g: g.then_far(2),
)


def fold(chunk):
    return jnp.concatenate([chunk[:HALF], chunk[HALF:]], axis=1)


class RingGather:
    def __init__(self, buf, place, stride, send, recv):
        self.buf, self.stride, self.send, self.recv = buf, stride, send, recv
        self.row, self.z = (place[1] * 4 + place[0]) * 2 + place[2], place[3]
        self.part = buf.shape[1] // PIECES
        self.far = NZ // stride // 2

    def plane(self, d):
        return lax.rem(self.z + d * self.stride + 2 * NZ, NZ)

    def copy(self, way, s, j):
        ref = self.buf.at[self.plane(1 - s if way == 0 else s - 1) // self.stride, pl.ds(j * self.part, self.part), :]
        device = {"row": self.row, "col": self.plane(1 if way == 0 else -1)}
        return remote(ref, self.send, self.recv.at[way, s, j], device)

    def wait(self, way, s, j):
        ref = self.buf.at[self.plane(-s if way == 0 else s) // self.stride, pl.ds(j * self.part, self.part), :]
        device = {"row": self.row, "col": self.plane(1)}
        remote(ref, self.send, self.recv.at[way, s, j], device).wait_recv()

    def pieces(self, last):
        for j in range(PIECES):
            for way in range(2):
                if not last or (way == 0) == (j < 3):
                    yield way, j

    def step(self, s, first=False, last=False):
        for way, j in self.pieces(last):
            if not first:
                self.wait(way, s - 1, j)
            self.copy(way, s, j).start()
        if last:
            for way, j in self.pieces(False):
                if (way == 0) != (j < 3):
                    self.wait(way, s - 1, j)

    def end(self):
        for way, j in self.pieces(True):
            self.wait(way, self.far, j)


def kernel(
    x_ref, out_ref,
    slab, xrow, xcol, gram, square, grow, gcol, mrow,
    sent, sr, xr, br, gr, cr, mr,
):
    row, z = lax.axis_index("row"), lax.axis_index("col")
    core = lax.rem(row, 2)
    x = lax.rem(row // 2, 4)
    y = row // 8
    place = (x, y, core, z)
    me = core * 16 + y * 4 + x
    up = {"row": row, "col": lax.rem(z + 1, NZ)}
    down = {"row": row, "col": lax.rem(z + NZ - 1, NZ)}

    def line(q):
        return q // 2

    def half(q):
        return pl.ds(pl.multiple_of(lax.rem(q, 2) * HALF, 16), HALF)

    gather_x = [
        PlaneGather(
            w, place, lambda i, w=w: slab.at[w, i], HALF, BLOCK, sent.at[0], sr.at[w]
        )
        for w in range(2)
    ]
    gather_c = [
        PlaneGather(
            w, place, lambda i, w=w: gcol.at[i, pl.ds(w * HALF, HALF), :], CUT, HALF, sent.at[8], cr.at[w]
        )
        for w in range(2)
    ]
    ring_x = RingGather(xrow, place, 1, sent.at[1], xr)
    ring_g = RingGather(grow, place, 1, sent.at[9], gr)
    ring_m = RingGather(mrow, place, 1, sent.at[10], mr)
    g0 = gather_x[0]
    east, west, north, south = g0.device(1, 0), g0.device(-1, 0), g0.device(0, 1), g0.device(0, -1)
    east2, north2 = g0.device(2, 0), g0.device(0, 2)
    sibling = g0.sibling()

    barrier = pltpu.get_barrier_semaphore()
    for device in (east, west, north, south, sibling, up, down):
        pl.semaphore_signal(barrier, inc=1, device_id=device, device_id_type=MESH)
    xrow[z] = x_ref[...].astype(jnp.bfloat16)
    slab[0, me] = x_ref[:, 0:256].astype(jnp.bfloat16)
    slab[1, me] = x_ref[:, 256:512].astype(jnp.bfloat16)
    gram[...] = jnp.zeros_like(gram)
    pl.semaphore_wait(barrier, 7)

    hands = core == line(z) // 4
    b = lax.rem(y + 4 - lax.rem(line(z), 4), 4)
    left, right = lax.rem(x + 3, 4), lax.rem(x + 1, 4)
    across = lax.rem(x + 2, 4)

    def whole(q, i):
        return xcol.at[q, i]

    def upper(q, i):
        return xcol.at[q, i, pl.ds(0, CUT), :]

    def lower(q, i):
        return xcol.at[q, i, pl.ds(CUT, HALF - CUT), :]

    def share(q, i):
        remote(whole(q, i), sent.at[7], br.at[q, 6], sibling).start()

    def spread(q, straight):
        @pl.when(straight)
        def _():
            remote(whole(q, x), sent.at[12], br.at[q, 4], east2).start()

        remote(whole(q, x), sent.at[4], br.at[q, 2], east).start()
        remote(whole(q, x), sent.at[5], br.at[q, 3], west).start()
        share(q, x)

    def source(q, straight):
        @pl.when(hands & (b == 0))
        def _():
            xcol[q, x] = xrow[q, half(z), :]

            @pl.when(straight)
            def _():
                remote(whole(q, x), sent.at[11], br.at[q, 0], north2).start()

            remote(whole(q, x), sent.at[2], br.at[q, 0], north).start()
            remote(whole(q, x), sent.at[3], br.at[q, 0], south).start()
            spread(q, straight)

    def relay(q, straight):
        @pl.when(hands & (lax.rem(b, 2) == 1))
        def _():
            remote(whole(q, x), sent.at[2], br.at[q, 0], north).wait_recv()

            @pl.when((b == 1) & jnp.logical_not(straight))
            def _():
                remote(upper(q, x), sent.at[2], br.at[q, 0], north).start()

            @pl.when((b == 3) & jnp.logical_not(straight))
            def _():
                remote(lower(q, x), sent.at[3], br.at[q, 1], south).start()

            spread(q, straight)

    def far(q, straight):
        @pl.when(hands & (b == 2))
        def _():
            @pl.when(straight)
            def _():
                remote(whole(q, x), sent.at[11], br.at[q, 0], north2).wait_recv()

            @pl.when(jnp.logical_not(straight))
            def _():
                remote(upper(q, x), sent.at[2], br.at[q, 0], north).wait_recv()
                remote(lower(q, x), sent.at[3], br.at[q, 1], south).wait_recv()

            spread(q, straight)

    def beside(q, straight):
        @pl.when(hands)
        def _():
            remote(whole(q, left), sent.at[4], br.at[q, 2], east).wait_recv()
            remote(whole(q, right), sent.at[5], br.at[q, 3], west).wait_recv()

            @pl.when(jnp.logical_not(straight))
            def _():
                remote(upper(q, left), sent.at[6], br.at[q, 4], east).start()
                remote(lower(q, right), sent.at[6], br.at[q, 5], west).start()

            share(q, left)
            share(q, right)

    def opposite(q, straight):
        @pl.when(hands)
        def _():
            @pl.when(straight)
            def _():
                remote(whole(q, across), sent.at[12], br.at[q, 4], east2).wait_recv()

            @pl.when(jnp.logical_not(straight))
            def _():
                remote(upper(q, across), sent.at[6], br.at[q, 4], east).wait_recv()
                remote(lower(q, across), sent.at[6], br.at[q, 5], west).wait_recv()

            share(q, across)

    def add(q, straight):
        @pl.when(jnp.logical_not(hands))
        def _():
            remote(xcol.at[q], sent.at[7], br.at[q, 6], sibling).wait_recv()

        gram[...] += lax.dot_general(
            xrow[q],
            xcol[q].reshape(WIDE, COLS),
            (((1,), (1,)), ((), ())),
            preferred_element_type=jnp.float32,
        )

    chain = (source, relay, far, beside, opposite, add)

    @pl.loop(0, NZ // 2 + len(chain))
    def _(t):
        @pl.when(t == 0)
        def _():
            ring_x.step(1, first=True)

        @pl.when((t > 0) & (t < 7))
        def _():
            ring_x.step(t + 1)

        @pl.when(t == 7)
        def _():
            ring_x.step(8, last=True)

        @pl.when(t == 8)
        def _():
            ring_x.end()

        for lag, action in enumerate(chain):
            n = t - lag

            @pl.when((n >= 0) & (n <= 8))
            def _(n=n, action=action):
                straight = n >= STRAIGHT
                action(lax.rem(z + n, NZ), straight)

                @pl.when((n > 0) & (n < 8))
                def _():
                    action(lax.rem(z + NZ - n, NZ), straight)

        for n, stage in enumerate(STAGES):

            @pl.when(t == n)
            def _(stage=stage):
                for g in gather_x:
                    stage(g)

    theirs = pl.ds((1 - core) * 16, 16)
    for g in gather_x:
        g.others(slab.at[g.way, theirs])

    gb = gram[...].astype(jnp.bfloat16)
    grow[z] = fold(gb)
    gcol[me] = gb
    square[...] = jnp.zeros_like(square)
    theirs = pl.ds((1 - core) * 16, 16)

    def unfold(ref, q):
        return jnp.concatenate([ref[q, :, 0:WIDE], ref[q, :, WIDE : 2 * WIDE]], axis=0)

    def square_step(d):
        q = lax.rem(z + d + NZ, NZ)
        square[...] += jnp.dot(
            unfold(grow, q),
            gcol[pl.ds(line(q) * 4, 4), half(q), :].reshape(WIDE, WIDE),
            preferred_element_type=jnp.float32,
        )

    ring_g.step(1, first=True)
    for s, stages in enumerate(((0,), (1,), (2, 3), (4, 5), (6, 7), (8, 9, 10)), 1):
        if s > 1:
            ring_g.step(s)
        for n in stages:
            for g in gather_c:
                STAGES[n](g)
    for w, g in enumerate(gather_c):
        g.others(gcol.at[theirs, pl.ds(w * HALF, HALF), :])

    @pl.loop(-2, 3)
    def _(d):
        square_step(d)

    ring_g.step(7)

    @pl.loop(3, 6)
    def _(d):
        square_step(d)
        square_step(-d)

    ring_g.step(8, last=True)
    for d in (6, -6, 7, -7):
        square_step(d)
    ring_g.end()
    square_step(8)

    mixed = (coef_b * gram[...] + coef_c * square[...]).astype(jnp.bfloat16)
    mrow[z] = fold(mixed)

    def product(d):
        q = lax.rem(z + d + NZ, NZ)
        left_rows = unfold(mrow, q)
        for h in range(2):
            out_ref[:, h * 256 : (h + 1) * 256] += jnp.dot(
                left_rows,
                slab[h, pl.ds(line(q) * 4, 4), half(q), :].reshape(WIDE, 256),
                preferred_element_type=jnp.float32,
            )

    ring_m.step(1, first=True)
    out_ref[...] = coef_a * x_ref[...]
    product(0)

    @pl.loop(2, 8)
    def _(s):
        ring_m.step(s)
        product(1 - s)
        product(s - 1)

    ring_m.step(8, last=True)
    product(-7)
    product(7)
    ring_m.end()
    product(8)
    out_ref[...] = (0.2 * math.sqrt(COLS * NZ)) * out_ref[...]

    def gone(k, ref):
        remote(ref, sent.at[k], sent.at[k], up).wait_send()

    gone(0, slab.at[:, pl.ds(0, 31)])
    gone(1, xrow.at[pl.ds(0, 15)])

    @pl.when(hands)
    def _():
        @pl.when(b == 0)
        def _():
            gone(2, xcol.at[:, 0])
            gone(3, xcol.at[:, 0])
            gone(11, xcol.at[pl.ds(0, LONG), 0])

        @pl.when(b == 1)
        def _():
            gone(2, xcol.at[pl.ds(0, NZ - LONG), 0, pl.ds(0, CUT), :])

        @pl.when(b == 3)
        def _():
            gone(3, xcol.at[pl.ds(0, NZ - LONG), 0, pl.ds(CUT, HALF - CUT), :])

        gone(4, xcol.at[:, 0])
        gone(5, xcol.at[:, 0])
        gone(6, xcol.at[pl.ds(0, NZ - LONG), 0])
        gone(7, xcol)
        gone(12, xcol.at[pl.ds(0, LONG), 0])

    gone(8, gcol.at[pl.ds(0, 31)])
    gone(9, grow.at[pl.ds(0, 15)])
    gone(10, mrow.at[pl.ds(0, 15)])


def local(iterate):
    dma = pltpu.SemaphoreType.DMA
    return pl.pallas_call(
        kernel,
        out_shape=jax.ShapeDtypeStruct((BLOCK, COLS), jnp.float32),
        in_specs=[pl.BlockSpec(memory_space=pltpu.VMEM)],
        out_specs=pl.BlockSpec(memory_space=pltpu.VMEM),
        scratch_shapes=[
            pltpu.VMEM((2, 32, BLOCK, 256), jnp.bfloat16),
            pltpu.VMEM((NZ, BLOCK, COLS), jnp.bfloat16),
            pltpu.VMEM((NZ, 4, HALF, COLS), jnp.bfloat16),
            pltpu.VMEM((BLOCK, WIDE), jnp.float32),
            pltpu.VMEM((BLOCK, WIDE), jnp.float32),
            pltpu.VMEM((NZ, HALF, 2 * WIDE), jnp.bfloat16),
            pltpu.VMEM((32, BLOCK, WIDE), jnp.bfloat16),
            pltpu.VMEM((NZ, HALF, 2 * WIDE), jnp.bfloat16),
            dma((13,)),
            dma((2, 21)),
            dma((2, 9, PIECES)),
            dma((NZ, 7)),
            dma((2, 9, PIECES)),
            dma((2, 21)),
            dma((2, 9, PIECES)),
        ],
        compiler_params=pltpu.CompilerParams(
            collective_id=0, has_side_effects=True, vmem_limit_bytes=48 * 1024 * 1024
        ),
        cost_estimate=pl.CostEstimate(
            flops=2300000000, bytes_accessed=700000, transcendentals=0
        ),
    )(iterate)


def solution(mesh):
    return jax.shard_map(
        local,
        mesh=mesh,
        in_specs=(P("row", "col"),),
        out_specs=P("row", "col"),
        check_vma=False,
    )
```

```python
import functools
import math

import jax
import jax.numpy as jnp
from jax import lax
from jax.experimental import pallas as pl
from jax.experimental.pallas import tpu as pltpu
from jax.sharding import PartitionSpec as P

coef_a = 3.4445
coef_b = -4.775
coef_c = 2.0315

NX = 4
NY = 4
NZ = 16
BLOCK = 160
HALF = 80
WIDE = 320
COLS = 512
CUT = 48
STRAIGHT = 8
LONG = 2 * (8 - STRAIGHT) + 1
PIECES = 5
SLOTS = 4
MESH = pl.DeviceIdType.MESH


def remote(ref, send_sem, recv_sem, device):
    return pltpu.make_async_remote_copy(
        src_ref=ref,
        dst_ref=ref,
        send_sem=send_sem,
        recv_sem=recv_sem,
        device_id=device,
        device_id_type=MESH,
    )


class PlaneGather:
    def __init__(self, way, place, view, cut, total, send, recv):
        self.way, self.place, self.view = way, place, view
        self.cuts = ((0, cut), (cut, total - cut))
        self.send, self.recv = send, recv

    def coords(self, a, b):
        x, y, _, _ = self.place
        dx, dy = (a, b) if self.way == 0 else (b, a)
        return lax.rem(x + (dx % 4), 4), lax.rem(y + (dy % 4), 4)

    def block(self, a, b, core=None):
        x, y = self.coords(a, b)
        core = self.place[2] if core is None else core
        return core * 16 + y * 4 + x

    def device(self, a, b):
        x, y = self.coords(a, b)
        return {"row": (y * 4 + x) * 2 + self.place[2], "col": self.place[3]}

    def sibling(self):
        x, y, core, z = self.place
        return {"row": (y * 4 + x) * 2 + 1 - core, "col": z}

    def half(self, index, part):
        start, size = self.cuts[part]
        return self.view(index).at[pl.ds(start, size), :]

    def push(self, a, b, to, slot, part=None):
        index = self.block(a, b)
        ref = self.view(index) if part is None else self.half(index, part)
        device = self.sibling() if to is None else self.device(*to)
        remote(ref, self.send, self.recv.at[slot], device).start()

    def wait(self, a, b, slot, part=None, core=None):
        index = self.block(a, b, core)
        ref = self.view(index) if part is None else self.half(index, part)
        remote(ref, self.send, self.recv.at[slot], self.sibling()).wait_recv()

    def second(self, a):
        k = a % 4
        self.push(a, 0, (0, 1), 4 + 2 * k)
        self.push(a, 0, (0, -1), 5 + 2 * k)

    def other(self, a, b):
        self.push(a, b, None, 20)

    def own(self):
        self.push(0, 0, (1, 0), 0)
        self.push(0, 0, (-1, 0), 1)
        self.second(0)
        self.other(0, 0)

    def first(self):
        self.wait(-1, 0, 0)
        self.push(-1, 0, (1, 0), 2, part=0)
        self.second(-1)
        self.wait(1, 0, 1)
        self.push(1, 0, (-1, 0), 3, part=1)
        self.second(1)
        self.other(-1, 0)
        self.other(1, 0)

    def first_far(self):
        self.wait(2, 0, 2, part=0)
        self.wait(2, 0, 3, part=1)
        self.second(2)
        self.other(2, 0)

    def then(self, a):
        k = a % 4
        self.wait(a, -1, 4 + 2 * k)
        self.push(a, -1, (0, 1), 12 + 2 * k, part=0)
        self.wait(a, 1, 5 + 2 * k)
        self.push(a, 1, (0, -1), 13 + 2 * k, part=1)
        self.other(a, -1)
        self.other(a, 1)

    def then_far(self, a):
        k = a % 4
        self.wait(a, 2, 12 + 2 * k, part=0)
        self.wait(a, 2, 13 + 2 * k, part=1)
        self.other(a, 2)

    def others(self, blocks):
        remote(blocks, self.send, self.recv.at[20], self.sibling()).wait_recv()


STAGES = (
    lambda g: g.own(),
    lambda g: g.first(),
    lambda g: g.then(0),
    lambda g: g.first_far(),
    lambda g: g.then(-1),
    lambda g: g.then(1),
    lambda g: g.then_far(0),
    lambda g: g.then(2),
    lambda g: g.then_far(-1),
    lambda g: g.then_far(1),
    lambda g: g.then_far(2),
)


def fold(chunk):
    return jnp.concatenate([chunk[:HALF], chunk[HALF:]], axis=1)


class RingGather:
    def __init__(self, buf, place, pieces, send, recv):
        self.buf, self.pieces, self.send, self.recv = buf, pieces, send, recv
        self.row, self.z = (place[1] * 4 + place[0]) * 2 + place[2], place[3]
        self.part = buf.shape[1] // pieces
        self.shared = (pieces + 1) // 2

    def plane(self, d):
        return lax.rem(self.z + d + 2 * NZ, NZ)

    def copy(self, way, s, j):
        ref = self.piece(1 - s if way == 0 else s - 1, j)
        device = {"row": self.row, "col": self.plane(1 if way == 0 else -1)}
        return remote(ref, self.send, self.recv.at[way, s % SLOTS if isinstance(s, int) else lax.rem(s, SLOTS), j], device)

    def wait(self, way, s, j):
        ref = self.piece(-s if way == 0 else s, j)
        device = {"row": self.row, "col": self.plane(1)}
        remote(ref, self.send, self.recv.at[way, s % SLOTS if isinstance(s, int) else lax.rem(s, SLOTS), j], device).wait_recv()

    def piece(self, d, j):
        return self.buf.at[self.plane(d), pl.ds(pl.multiple_of(j * self.part, 16), self.part), :]

    def step(self, s, first=False, last=False):
        @pl.loop(0, self.pieces)
        def _(j):
            for way in range(2):
                if not first:
                    self.wait(way, s - 1, j)
                if last:
                    pl.when((j < self.shared) == (way == 0))(self.copy(way, s, j).start)
                else:
                    self.copy(way, s, j).start()

    def end(self):
        @pl.loop(0, self.shared)
        def _(j):
            self.wait(0, NZ // 2, j)

        @pl.loop(self.shared, self.pieces)
        def _(j):
            self.wait(1, NZ // 2, j)


def kernel(
    x_ref, out_ref,
    slab, xrow, xcol, gram, square, grow, gcol, mrow,
    sent, sr, xr, br, gr, cr,
):
    row, z = lax.axis_index("row"), lax.axis_index("col")
    core = lax.rem(row, 2)
    x = lax.rem(row // 2, 4)
    y = row // 8
    place = (x, y, core, z)
    me = core * 16 + y * 4 + x
    up = {"row": row, "col": lax.rem(z + 1, NZ)}
    down = {"row": row, "col": lax.rem(z + NZ - 1, NZ)}

    def line(q):
        return q // 2

    def half(q):
        return pl.ds(pl.multiple_of(lax.rem(q, 2) * HALF, 16), HALF)

    gather_x = [
        PlaneGather(
            w, place, lambda i, w=w: slab.at[w, i], HALF, BLOCK, sent.at[0], sr.at[w]
        )
        for w in range(2)
    ]
    gather_c = [
        PlaneGather(
            w, place, lambda i, w=w: gcol.at[i, pl.ds(w * HALF, HALF), :], CUT, HALF, sent.at[8], cr.at[w]
        )
        for w in range(2)
    ]
    ring_x = RingGather(xrow, place, PIECES, sent.at[1], xr)
    ring_g = RingGather(grow, place, PIECES, sent.at[9], gr)
    ring_m = RingGather(mrow, place, PIECES, sent.at[10], xr)
    g0 = gather_x[0]
    east, west, north, south = g0.device(1, 0), g0.device(-1, 0), g0.device(0, 1), g0.device(0, -1)
    east2, north2 = g0.device(2, 0), g0.device(0, 2)
    sibling = g0.sibling()

    barrier = pltpu.get_barrier_semaphore()
    for device in (east, west, north, south, sibling, up, down):
        pl.semaphore_signal(barrier, inc=1, device_id=device, device_id_type=MESH)
    xrow[z] = x_ref[...].astype(jnp.bfloat16)
    slab[0, me] = x_ref[:, 0:256].astype(jnp.bfloat16)
    slab[1, me] = x_ref[:, 256:512].astype(jnp.bfloat16)
    gram[...] = jnp.zeros_like(gram)
    pl.semaphore_wait(barrier, 7)

    hands = core == line(z) // 4
    b = lax.rem(y + 4 - lax.rem(line(z), 4), 4)
    left, right = lax.rem(x + 3, 4), lax.rem(x + 1, 4)
    across = lax.rem(x + 2, 4)

    def whole(q, i):
        return xcol.at[q, i]

    def upper(q, i):
        return xcol.at[q, i, pl.ds(0, CUT), :]

    def lower(q, i):
        return xcol.at[q, i, pl.ds(CUT, HALF - CUT), :]

    def share(q, i):
        remote(whole(q, i), sent.at[7], br.at[q, 4], sibling).start()

    def spread(q, straight):
        @pl.when(straight)
        def _():
            remote(whole(q, x), sent.at[12], br.at[q, 3], east2).start()

        remote(whole(q, x), sent.at[4], br.at[q, 1], east).start()
        remote(whole(q, x), sent.at[5], br.at[q, 2], west).start()
        share(q, x)

    def source(q, straight):
        @pl.when(hands & (b == 0))
        def _():
            xcol[q, x] = xrow[q, half(z), :]

            @pl.when(straight)
            def _():
                remote(whole(q, x), sent.at[11], br.at[q, 0], north2).start()

            remote(whole(q, x), sent.at[2], br.at[q, 0], north).start()
            remote(whole(q, x), sent.at[3], br.at[q, 0], south).start()
            spread(q, straight)

    def relay(q, straight):
        @pl.when(hands & (lax.rem(b, 2) == 1))
        def _():
            remote(whole(q, x), sent.at[2], br.at[q, 0], north).wait_recv()

            @pl.when((b == 1) & jnp.logical_not(straight))
            def _():
                remote(upper(q, x), sent.at[2], br.at[q, 0], north).start()

            @pl.when((b == 3) & jnp.logical_not(straight))
            def _():
                remote(lower(q, x), sent.at[3], br.at[q, 0], south).start()

            spread(q, straight)

    def far(q, straight):
        @pl.when(hands & (b == 2))
        def _():
            remote(whole(q, x), sent.at[2], br.at[q, 0], north).wait_recv()
            spread(q, straight)

    def beside(q, straight):
        @pl.when(hands)
        def _():
            remote(whole(q, left), sent.at[4], br.at[q, 1], east).wait_recv()
            remote(whole(q, right), sent.at[5], br.at[q, 2], west).wait_recv()

            @pl.when(jnp.logical_not(straight))
            def _():
                remote(upper(q, left), sent.at[6], br.at[q, 3], east).start()
                remote(lower(q, right), sent.at[6], br.at[q, 3], west).start()

            share(q, left)
            share(q, right)

    def opposite(q, straight):
        @pl.when(hands)
        def _():
            remote(whole(q, across), sent.at[6], br.at[q, 3], east).wait_recv()
            share(q, across)

    def add(q, straight):
        @pl.when(jnp.logical_not(hands))
        def _():
            remote(xcol.at[q], sent.at[7], br.at[q, 4], sibling).wait_recv()

        gram[...] += lax.dot_general(
            xrow[q],
            xcol[q].reshape(WIDE, COLS),
            (((1,), (1,)), ((), ())),
            preferred_element_type=jnp.float32,
        )

    chain = (source, relay, far, beside, opposite, add)

    @pl.loop(0, NZ // 2 + len(chain))
    def _(t):
        @pl.when(t == 0)
        def _():
            ring_x.step(1, first=True)

        @pl.when((t > 0) & (t < 7))
        def _():
            ring_x.step(t + 1)

        @pl.when(t == 7)
        def _():
            ring_x.step(8, last=True)

        @pl.when(t == 8)
        def _():
            ring_x.end()

        for lag, action in enumerate(chain):
            n = t - lag

            both = (n > 0) & (n < 8)

            @pl.loop(0, jnp.where((n >= 0) & (n <= 8), jnp.where(both, 2, 1), 0))
            def _(side, n=n, action=action):
                action(lax.rem(z + jnp.where(side == 0, n, NZ - n), NZ), n >= STRAIGHT)

        for n, stage in enumerate(STAGES):

            @pl.when(t == n)
            def _(stage=stage):
                for g in gather_x:
                    stage(g)

    theirs = pl.ds((1 - core) * 16, 16)
    for g in gather_x:
        g.others(slab.at[g.way, theirs])

    gb = gram[...].astype(jnp.bfloat16)
    grow[z] = fold(gb)
    gcol[me] = gb
    square[...] = jnp.zeros_like(square)
    theirs = pl.ds((1 - core) * 16, 16)

    def unfold(ref, q):
        return jnp.concatenate([ref[q, :, 0:WIDE], ref[q, :, WIDE : 2 * WIDE]], axis=0)

    def square_step(d):
        q = lax.rem(z + d + NZ, NZ)
        square[...] += jnp.dot(
            unfold(grow, q),
            gcol[pl.ds(line(q) * 4, 4), half(q), :].reshape(WIDE, WIDE),
            preferred_element_type=jnp.float32,
        )

    ring_g.step(1, first=True)
    for s, stages in enumerate(((0,), (1,), (2, 3), (4, 5), (6, 7), (8, 9, 10)), 1):
        if s > 1:
            ring_g.step(s)
        for n in stages:
            for g in gather_c:
                STAGES[n](g)
    for w, g in enumerate(gather_c):
        g.others(gcol.at[theirs, pl.ds(w * HALF, HALF), :])

    @pl.loop(-2, 3)
    def _(d):
        square_step(d)

    ring_g.step(7)

    @pl.loop(3, 6)
    def _(d):
        square_step(d)
        square_step(-d)

    ring_g.step(8, last=True)
    for d in (6, -6, 7, -7):
        square_step(d)
    ring_g.end()
    square_step(8)

    mixed = (coef_b * gram[...] + coef_c * square[...]).astype(jnp.bfloat16)
    mrow[z] = fold(mixed)

    def product(d):
        q = lax.rem(z + d + NZ, NZ)
        left_rows = unfold(mrow, q)
        for h in range(2):
            out_ref[:, h * 256 : (h + 1) * 256] += jnp.dot(
                left_rows,
                slab[h, pl.ds(line(q) * 4, 4), half(q), :].reshape(WIDE, 256),
                preferred_element_type=jnp.float32,
            )

    ring_m.step(1, first=True)
    out_ref[...] = coef_a * x_ref[...]
    product(0)

    @pl.loop(2, 8)
    def _(s):
        ring_m.step(s)
        product(1 - s)
        product(s - 1)

    ring_m.step(8, last=True)
    product(-7)
    product(7)
    ring_m.end()
    product(8)
    out_ref[...] = (0.2 * math.sqrt(COLS * NZ)) * out_ref[...]

    def gone(k, ref):
        remote(ref, sent.at[k], sent.at[k], up).wait_send()

    gone(0, slab.at[:, pl.ds(0, 31)])
    gone(1, xrow.at[pl.ds(0, 15)])

    @pl.when(hands)
    def _():
        @pl.when(b == 0)
        def _():
            gone(2, xcol.at[:, 0])
            gone(3, xcol.at[:, 0])
            gone(11, xcol.at[pl.ds(0, LONG), 0])

        @pl.when(b == 1)
        def _():
            gone(2, xcol.at[pl.ds(0, NZ - LONG), 0, pl.ds(0, CUT), :])

        @pl.when(b == 3)
        def _():
            gone(3, xcol.at[pl.ds(0, NZ - LONG), 0, pl.ds(CUT, HALF - CUT), :])

        gone(4, xcol.at[:, 0])
        gone(5, xcol.at[:, 0])
        gone(6, xcol.at[pl.ds(0, NZ - LONG), 0])
        gone(7, xcol)
        gone(12, xcol.at[pl.ds(0, LONG), 0])

    gone(8, gcol.at[pl.ds(0, 31)])
    gone(9, grow.at[pl.ds(0, 15)])
    gone(10, mrow.at[pl.ds(0, 15)])


def local(iterate):
    dma = pltpu.SemaphoreType.DMA
    return pl.pallas_call(
        kernel,
        out_shape=jax.ShapeDtypeStruct((BLOCK, COLS), jnp.float32),
        in_specs=[pl.BlockSpec(memory_space=pltpu.VMEM)],
        out_specs=pl.BlockSpec(memory_space=pltpu.VMEM),
        scratch_shapes=[
            pltpu.VMEM((2, 32, BLOCK, 256), jnp.bfloat16),
            pltpu.VMEM((NZ, BLOCK, COLS), jnp.bfloat16),
            pltpu.VMEM((NZ, 4, HALF, COLS), jnp.bfloat16),
            pltpu.VMEM((BLOCK, WIDE), jnp.float32),
            pltpu.VMEM((BLOCK, WIDE), jnp.float32),
            pltpu.VMEM((NZ, HALF, 2 * WIDE), jnp.bfloat16),
            pltpu.VMEM((32, BLOCK, WIDE), jnp.bfloat16),
            pltpu.VMEM((NZ, HALF, 2 * WIDE), jnp.bfloat16),
            dma((13,)),
            dma((2, 21)),
            dma((2, SLOTS, PIECES)),
            dma((NZ, 5)),
            dma((2, SLOTS, PIECES)),
            dma((2, 21)),
        ],
        compiler_params=pltpu.CompilerParams(
            collective_id=0, has_side_effects=True, vmem_limit_bytes=48 * 1024 * 1024
        ),
        cost_estimate=pl.CostEstimate(
            flops=2300000000, bytes_accessed=700000, transcendentals=0
        ),
    )(iterate)


def solution(mesh):
    return jax.shard_map(
        local,
        mesh=mesh,
        in_specs=(P("row", "col"),),
        out_specs=P("row", "col"),
        check_vma=False,
    )
```

```python
import functools
import math

import jax
import jax.numpy as jnp
from jax import lax
from jax.experimental import pallas as pl
from jax.experimental.pallas import tpu as pltpu
from jax.sharding import PartitionSpec as P

coef_a = 3.4445
coef_b = -4.775
coef_c = 2.0315

NX = 4
NY = 4
NZ = 16
BLOCK = 160
HALF = 80
WIDE = 320
COLS = 512
CUT = 48
STRAIGHT = 8
LONG = 2 * (8 - STRAIGHT) + 1
PIECES = 5
SLOTS = 4
MESH = pl.DeviceIdType.MESH


def remote(ref, send_sem, recv_sem, device):
    return pltpu.make_async_remote_copy(
        src_ref=ref,
        dst_ref=ref,
        send_sem=send_sem,
        recv_sem=recv_sem,
        device_id=device,
        device_id_type=MESH,
    )


class PlaneGather:
    def __init__(self, way, place, view, cut, total, send, recv):
        self.way, self.place, self.view = way, place, view
        self.cuts = ((0, cut), (cut, total - cut))
        self.send, self.recv = send, recv

    def coords(self, a, b):
        x, y, _, _ = self.place
        dx, dy = (a, b) if self.way == 0 else (b, a)
        return lax.rem(x + (dx % 4), 4), lax.rem(y + (dy % 4), 4)

    def block(self, a, b, core=None):
        x, y = self.coords(a, b)
        core = self.place[2] if core is None else core
        return core * 16 + y * 4 + x

    def device(self, a, b):
        x, y = self.coords(a, b)
        return {"row": (y * 4 + x) * 2 + self.place[2], "col": self.place[3]}

    def sibling(self):
        x, y, core, z = self.place
        return {"row": (y * 4 + x) * 2 + 1 - core, "col": z}

    def half(self, index, part):
        start, size = self.cuts[part]
        return self.view(index).at[pl.ds(start, size), :]

    def push(self, a, b, to, slot, part=None):
        index = self.block(a, b)
        ref = self.view(index) if part is None else self.half(index, part)
        device = self.sibling() if to is None else self.device(*to)
        remote(ref, self.send, self.recv.at[slot], device).start()

    def wait(self, a, b, slot, part=None, core=None):
        index = self.block(a, b, core)
        ref = self.view(index) if part is None else self.half(index, part)
        remote(ref, self.send, self.recv.at[slot], self.sibling()).wait_recv()

    def second(self, a):
        k = a % 4
        self.push(a, 0, (0, 1), 4 + 2 * k)
        self.push(a, 0, (0, -1), 5 + 2 * k)

    def other(self, a, b):
        self.push(a, b, None, 20)

    def own(self):
        self.push(0, 0, (1, 0), 0)
        self.push(0, 0, (-1, 0), 1)
        self.second(0)
        self.other(0, 0)

    def first(self):
        self.wait(-1, 0, 0)
        self.push(-1, 0, (1, 0), 2, part=0)
        self.second(-1)
        self.wait(1, 0, 1)
        self.push(1, 0, (-1, 0), 3, part=1)
        self.second(1)
        self.other(-1, 0)
        self.other(1, 0)

    def first_far(self):
        self.wait(2, 0, 2, part=0)
        self.wait(2, 0, 3, part=1)
        self.second(2)
        self.other(2, 0)

    def then(self, a):
        k = a % 4
        self.wait(a, -1, 4 + 2 * k)
        self.push(a, -1, (0, 1), 12 + 2 * k, part=0)
        self.wait(a, 1, 5 + 2 * k)
        self.push(a, 1, (0, -1), 13 + 2 * k, part=1)
        self.other(a, -1)
        self.other(a, 1)

    def then_far(self, a):
        k = a % 4
        self.wait(a, 2, 12 + 2 * k, part=0)
        self.wait(a, 2, 13 + 2 * k, part=1)
        self.other(a, 2)

    def others(self, blocks):
        remote(blocks, self.send, self.recv.at[20], self.sibling()).wait_recv()


STAGES = (
    lambda g: g.own(),
    lambda g: g.first(),
    lambda g: g.then(0),
    lambda g: g.first_far(),
    lambda g: g.then(-1),
    lambda g: g.then(1),
    lambda g: g.then_far(0),
    lambda g: g.then(2),
    lambda g: g.then_far(-1),
    lambda g: g.then_far(1),
    lambda g: g.then_far(2),
)


SLAB = 8
WHEN = ((0,), (1,), (2,), (3, 4, 5), (6, 7), (8, 9, 10))


def fold(chunk):
    return jnp.concatenate([chunk[:HALF], chunk[HALF:]], axis=1)


class RingGather:
    def __init__(self, buf, place, pieces, send, recv):
        self.buf, self.pieces, self.send, self.recv = buf, pieces, send, recv
        self.row, self.z = (place[1] * 4 + place[0]) * 2 + place[2], place[3]
        self.part = buf.shape[1] // pieces
        self.shared = (pieces + 1) // 2

    def plane(self, d):
        return lax.rem(self.z + d + 2 * NZ, NZ)

    def copy(self, way, s, j):
        ref = self.piece(1 - s if way == 0 else s - 1, j)
        device = {"row": self.row, "col": self.plane(1 if way == 0 else -1)}
        return remote(ref, self.send, self.recv.at[way, s % SLOTS if isinstance(s, int) else lax.rem(s, SLOTS), j], device)

    def wait(self, way, s, j):
        ref = self.piece(-s if way == 0 else s, j)
        device = {"row": self.row, "col": self.plane(1)}
        remote(ref, self.send, self.recv.at[way, s % SLOTS if isinstance(s, int) else lax.rem(s, SLOTS), j], device).wait_recv()

    def piece(self, d, j):
        return self.buf.at[self.plane(d), pl.ds(pl.multiple_of(j * self.part, 16), self.part), :]

    def step(self, s, first=False, last=False):
        @pl.loop(0, self.pieces)
        def _(j):
            for way in range(2):
                if not first:
                    self.wait(way, s - 1, j)
                if last:
                    pl.when((j < self.shared) == (way == 0))(self.copy(way, s, j).start)
                else:
                    self.copy(way, s, j).start()

    def end(self):
        @pl.loop(0, self.shared)
        def _(j):
            self.wait(0, NZ // 2, j)

        @pl.loop(self.shared, self.pieces)
        def _(j):
            self.wait(1, NZ // 2, j)


def kernel(
    x_ref, out_ref,
    slab, xrow, xcol, gram, square, grow, gcol, mrow,
    sent, sr, xr, br, gr, cr,
):
    row, z = lax.axis_index("row"), lax.axis_index("col")
    core = lax.rem(row, 2)
    x = lax.rem(row // 2, 4)
    y = row // 8
    place = (x, y, core, z)
    me = core * 16 + y * 4 + x
    up = {"row": row, "col": lax.rem(z + 1, NZ)}
    down = {"row": row, "col": lax.rem(z + NZ - 1, NZ)}

    def line(q):
        return q // 2

    def half(q):
        return pl.ds(pl.multiple_of(lax.rem(q, 2) * HALF, 16), HALF)

    gather_x = [
        PlaneGather(
            w, place, lambda i, w=w: slab.at[w, i], HALF, BLOCK, sent.at[0], sr.at[w]
        )
        for w in range(2)
    ]
    gather_c = [
        PlaneGather(
            w, place, lambda i, w=w: gcol.at[i, pl.ds(w * HALF, HALF), :], CUT, HALF, sent.at[8], cr.at[w]
        )
        for w in range(2)
    ]
    ring_x = RingGather(xrow, place, PIECES, sent.at[1], xr)
    ring_g = RingGather(grow, place, PIECES, sent.at[9], gr)
    ring_m = RingGather(mrow, place, PIECES, sent.at[10], xr)
    g0 = gather_x[0]
    east, west, north, south = g0.device(1, 0), g0.device(-1, 0), g0.device(0, 1), g0.device(0, -1)
    east2, north2 = g0.device(2, 0), g0.device(0, 2)
    sibling = g0.sibling()

    barrier = pltpu.get_barrier_semaphore()
    for device in (east, west, north, south, sibling, up, down):
        pl.semaphore_signal(barrier, inc=1, device_id=device, device_id_type=MESH)
    xrow[z] = x_ref[...].astype(jnp.bfloat16)
    slab[0, me] = x_ref[:, 0:256].astype(jnp.bfloat16)
    slab[1, me] = x_ref[:, 256:512].astype(jnp.bfloat16)
    gram[...] = jnp.zeros_like(gram)
    pl.semaphore_wait(barrier, 7)

    hands = core == line(z) // 4
    b = lax.rem(y + 4 - lax.rem(line(z), 4), 4)
    left, right = lax.rem(x + 3, 4), lax.rem(x + 1, 4)
    across = lax.rem(x + 2, 4)

    def whole(q, i):
        return xcol.at[q, i]

    def upper(q, i):
        return xcol.at[q, i, pl.ds(0, CUT), :]

    def lower(q, i):
        return xcol.at[q, i, pl.ds(CUT, HALF - CUT), :]

    def share(q, i):
        remote(whole(q, i), sent.at[7], br.at[q, 4], sibling).start()

    def spread(q, straight):
        @pl.when(straight)
        def _():
            remote(whole(q, x), sent.at[12], br.at[q, 3], east2).start()

        remote(whole(q, x), sent.at[4], br.at[q, 1], east).start()
        remote(whole(q, x), sent.at[5], br.at[q, 2], west).start()
        share(q, x)

    def source(q, straight):
        @pl.when(hands & (b == 0))
        def _():
            xcol[q, x] = xrow[q, half(z), :]

            @pl.when(straight)
            def _():
                remote(whole(q, x), sent.at[11], br.at[q, 0], north2).start()

            remote(whole(q, x), sent.at[2], br.at[q, 0], north).start()
            remote(whole(q, x), sent.at[3], br.at[q, 0], south).start()
            spread(q, straight)

    def relay(q, straight):
        @pl.when(hands & (lax.rem(b, 2) == 1))
        def _():
            remote(whole(q, x), sent.at[2], br.at[q, 0], north).wait_recv()

            @pl.when((b == 1) & jnp.logical_not(straight))
            def _():
                remote(upper(q, x), sent.at[2], br.at[q, 0], north).start()

            @pl.when((b == 3) & jnp.logical_not(straight))
            def _():
                remote(lower(q, x), sent.at[3], br.at[q, 0], south).start()

            spread(q, straight)

    def far(q, straight):
        @pl.when(hands & (b == 2))
        def _():
            remote(whole(q, x), sent.at[2], br.at[q, 0], north).wait_recv()
            spread(q, straight)

    def beside(q, straight):
        @pl.when(hands)
        def _():
            remote(whole(q, left), sent.at[4], br.at[q, 1], east).wait_recv()
            remote(whole(q, right), sent.at[5], br.at[q, 2], west).wait_recv()

            @pl.when(jnp.logical_not(straight))
            def _():
                remote(upper(q, left), sent.at[6], br.at[q, 3], east).start()
                remote(lower(q, right), sent.at[6], br.at[q, 3], west).start()

            share(q, left)
            share(q, right)

    def opposite(q, straight):
        @pl.when(hands)
        def _():
            remote(whole(q, across), sent.at[6], br.at[q, 3], east).wait_recv()
            share(q, across)

    def add(q, straight):
        @pl.when(jnp.logical_not(hands))
        def _():
            remote(xcol.at[q], sent.at[7], br.at[q, 4], sibling).wait_recv()

        gram[...] += lax.dot_general(
            xrow[q],
            xcol[q].reshape(WIDE, COLS),
            (((1,), (1,)), ((), ())),
            preferred_element_type=jnp.float32,
        )

    chain = (source, relay, far, beside, opposite, add)

    @pl.loop(0, NZ // 2 + len(chain))
    def _(t):
        @pl.when(t == 0)
        def _():
            ring_x.step(1, first=True)

        @pl.when((t > 0) & (t < 7))
        def _():
            ring_x.step(t + 1)

        @pl.when(t == 7)
        def _():
            ring_x.step(8, last=True)

        @pl.when(t == 8)
        def _():
            ring_x.end()

        for lag, action in enumerate(chain):
            n = t - lag

            both = (n > 0) & (n < 8)

            @pl.loop(0, jnp.where((n >= 0) & (n <= 8), jnp.where(both, 2, 1), 0))
            def _(side, n=n, action=action):
                action(lax.rem(z + jnp.where(side == 0, n, NZ - n), NZ), n >= STRAIGHT)

        for n, stage in enumerate(STAGES[:SLAB]):

            @pl.when(t == n)
            def _(stage=stage):
                for g in gather_x:
                    stage(g)

    gb = gram[...].astype(jnp.bfloat16)
    grow[z] = fold(gb)
    gcol[me] = gb
    square[...] = jnp.zeros_like(square)
    theirs = pl.ds((1 - core) * 16, 16)

    def unfold(ref, q):
        return jnp.concatenate([ref[q, :, 0:WIDE], ref[q, :, WIDE : 2 * WIDE]], axis=0)

    def square_step(d):
        q = lax.rem(z + d + NZ, NZ)
        square[...] += jnp.dot(
            unfold(grow, q),
            gcol[pl.ds(line(q) * 4, 4), half(q), :].reshape(WIDE, WIDE),
            preferred_element_type=jnp.float32,
        )

    ring_g.step(1, first=True)
    for s, stages in enumerate(WHEN, 1):
        if s > 1:
            ring_g.step(s)
        for n in stages:
            for g in gather_c:
                STAGES[n](g)
        if s == 2:
            for stage in STAGES[SLAB:]:
                for g in gather_x:
                    stage(g)
    ring_g.step(7)
    for w, g in enumerate(gather_c):
        g.others(gcol.at[theirs, pl.ds(w * HALF, HALF), :])

    @pl.loop(-2, 3)
    def _(d):
        square_step(d)

    ring_g.step(8, last=True)

    @pl.loop(3, 8)
    def _(d):
        square_step(d)
        square_step(-d)

    ring_g.end()
    square_step(8)

    mixed = (coef_b * gram[...] + coef_c * square[...]).astype(jnp.bfloat16)
    mrow[z] = fold(mixed)

    def product(d):
        q = lax.rem(z + d + NZ, NZ)
        left_rows = unfold(mrow, q)
        for h in range(2):
            out_ref[:, h * 256 : (h + 1) * 256] += jnp.dot(
                left_rows,
                slab[h, pl.ds(line(q) * 4, 4), half(q), :].reshape(WIDE, 256),
                preferred_element_type=jnp.float32,
            )

    ring_m.step(1, first=True)
    for g in gather_x:
        g.others(slab.at[g.way, theirs])
    out_ref[...] = coef_a * x_ref[...]
    product(0)

    @pl.loop(2, 8)
    def _(s):
        ring_m.step(s)
        product(1 - s)
        product(s - 1)

    ring_m.step(8, last=True)
    product(-7)
    product(7)
    ring_m.end()
    product(8)
    out_ref[...] = (0.2 * math.sqrt(COLS * NZ)) * out_ref[...]

    def gone(k, ref):
        remote(ref, sent.at[k], sent.at[k], up).wait_send()

    gone(0, slab.at[:, pl.ds(0, 31)])
    gone(1, xrow.at[pl.ds(0, 15)])

    @pl.when(hands)
    def _():
        @pl.when(b == 0)
        def _():
            gone(2, xcol.at[:, 0])
            gone(3, xcol.at[:, 0])
            gone(11, xcol.at[pl.ds(0, LONG), 0])

        @pl.when(b == 1)
        def _():
            gone(2, xcol.at[pl.ds(0, NZ - LONG), 0, pl.ds(0, CUT), :])

        @pl.when(b == 3)
        def _():
            gone(3, xcol.at[pl.ds(0, NZ - LONG), 0, pl.ds(CUT, HALF - CUT), :])

        gone(4, xcol.at[:, 0])
        gone(5, xcol.at[:, 0])
        gone(6, xcol.at[pl.ds(0, NZ - LONG), 0])
        gone(7, xcol)
        gone(12, xcol.at[pl.ds(0, LONG), 0])

    gone(8, gcol.at[pl.ds(0, 31)])
    gone(9, grow.at[pl.ds(0, 15)])
    gone(10, mrow.at[pl.ds(0, 15)])


def local(iterate):
    dma = pltpu.SemaphoreType.DMA
    return pl.pallas_call(
        kernel,
        out_shape=jax.ShapeDtypeStruct((BLOCK, COLS), jnp.float32),
        in_specs=[pl.BlockSpec(memory_space=pltpu.VMEM)],
        out_specs=pl.BlockSpec(memory_space=pltpu.VMEM),
        scratch_shapes=[
            pltpu.VMEM((2, 32, BLOCK, 256), jnp.bfloat16),
            pltpu.VMEM((NZ, BLOCK, COLS), jnp.bfloat16),
            pltpu.VMEM((NZ, 4, HALF, COLS), jnp.bfloat16),
            pltpu.VMEM((BLOCK, WIDE), jnp.float32),
            pltpu.VMEM((BLOCK, WIDE), jnp.float32),
            pltpu.VMEM((NZ, HALF, 2 * WIDE), jnp.bfloat16),
            pltpu.VMEM((32, BLOCK, WIDE), jnp.bfloat16),
            pltpu.VMEM((NZ, HALF, 2 * WIDE), jnp.bfloat16),
            dma((13,)),
            dma((2, 21)),
            dma((2, SLOTS, PIECES)),
            dma((NZ, 5)),
            dma((2, SLOTS, PIECES)),
            dma((2, 21)),
        ],
        compiler_params=pltpu.CompilerParams(
            collective_id=0, has_side_effects=True, vmem_limit_bytes=48 * 1024 * 1024
        ),
        cost_estimate=pl.CostEstimate(
            flops=2300000000, bytes_accessed=700000, transcendentals=0
        ),
    )(iterate)


def solution(mesh):
    return jax.shard_map(
        local,
        mesh=mesh,
        in_specs=(P("row", "col"),),
        out_specs=P("row", "col"),
        check_vma=False,
    )
```

```python
import functools
import math

import jax
import jax.numpy as jnp
from jax import lax
from jax.experimental import pallas as pl
from jax.experimental.pallas import tpu as pltpu
from jax.sharding import PartitionSpec as P

coef_a = 3.4445
coef_b = -4.775
coef_c = 2.0315

NX = 4
NY = 4
NZ = 16
BLOCK = 160
HALF = 80
WIDE = 320
COLS = 512
CUT = 48
STRAIGHT = 8
LONG = 2 * (8 - STRAIGHT) + 1
PIECES = 5
SLOTS = 4
MESH = pl.DeviceIdType.MESH


def remote(ref, send_sem, recv_sem, device):
    return pltpu.make_async_remote_copy(
        src_ref=ref,
        dst_ref=ref,
        send_sem=send_sem,
        recv_sem=recv_sem,
        device_id=device,
        device_id_type=MESH,
    )


class PlaneGather:
    def __init__(self, way, place, view, cut, total, send, recv):
        self.way, self.place, self.view = way, place, view
        self.cuts = ((0, cut), (cut, total - cut))
        self.send, self.recv = send, recv

    def coords(self, a, b):
        x, y, _, _ = self.place
        dx, dy = (a, b) if self.way == 0 else (b, a)
        return lax.rem(x + (dx % 4), 4), lax.rem(y + (dy % 4), 4)

    def block(self, a, b, core=None):
        x, y = self.coords(a, b)
        core = self.place[2] if core is None else core
        return core * 16 + y * 4 + x

    def device(self, a, b):
        x, y = self.coords(a, b)
        return {"row": (y * 4 + x) * 2 + self.place[2], "col": self.place[3]}

    def sibling(self):
        x, y, core, z = self.place
        return {"row": (y * 4 + x) * 2 + 1 - core, "col": z}

    def half(self, index, part):
        start, size = self.cuts[part]
        return self.view(index).at[pl.ds(start, size), :]

    def push(self, a, b, to, slot, part=None):
        index = self.block(a, b)
        ref = self.view(index) if part is None else self.half(index, part)
        device = self.sibling() if to is None else self.device(*to)
        remote(ref, self.send, self.recv.at[slot], device).start()

    def wait(self, a, b, slot, part=None, core=None):
        index = self.block(a, b, core)
        ref = self.view(index) if part is None else self.half(index, part)
        remote(ref, self.send, self.recv.at[slot], self.sibling()).wait_recv()

    def second(self, a):
        k = a % 4
        self.push(a, 0, (0, 1), 4 + 2 * k)
        self.push(a, 0, (0, -1), 5 + 2 * k)

    def other(self, a, b):
        self.push(a, b, None, 20)

    def own(self):
        self.push(0, 0, (1, 0), 0)
        self.push(0, 0, (-1, 0), 1)
        self.second(0)
        self.other(0, 0)

    def first(self):
        self.wait(-1, 0, 0)
        self.push(-1, 0, (1, 0), 2, part=0)
        self.second(-1)
        self.wait(1, 0, 1)
        self.push(1, 0, (-1, 0), 3, part=1)
        self.second(1)
        self.other(-1, 0)
        self.other(1, 0)

    def first_far(self):
        self.wait(2, 0, 2, part=0)
        self.wait(2, 0, 3, part=1)
        self.second(2)
        self.other(2, 0)

    def then(self, a):
        k = a % 4
        self.wait(a, -1, 4 + 2 * k)
        self.push(a, -1, (0, 1), 12 + 2 * k, part=0)
        self.wait(a, 1, 5 + 2 * k)
        self.push(a, 1, (0, -1), 13 + 2 * k, part=1)
        self.other(a, -1)
        self.other(a, 1)

    def then_far(self, a):
        k = a % 4
        self.wait(a, 2, 12 + 2 * k, part=0)
        self.wait(a, 2, 13 + 2 * k, part=1)
        self.other(a, 2)

    def others(self, blocks):
        remote(blocks, self.send, self.recv.at[20], self.sibling()).wait_recv()


STAGES = (
    lambda g: g.own(),
    lambda g: g.first(),
    lambda g: g.then(0),
    lambda g: g.first_far(),
    lambda g: g.then(-1),
    lambda g: g.then(1),
    lambda g: g.then_far(0),
    lambda g: g.then(2),
    lambda g: g.then_far(-1),
    lambda g: g.then_far(1),
    lambda g: g.then_far(2),
)


SLAB = 9
WHEN = ((0,), (1,), (2,), (3, 4, 5), (6, 7), (8, 9, 10))


def fold(chunk):
    return jnp.concatenate([chunk[:HALF], chunk[HALF:]], axis=1)


class RingGather:
    def __init__(self, buf, place, pieces, send, recv):
        self.buf, self.pieces, self.send, self.recv = buf, pieces, send, recv
        self.row, self.z = (place[1] * 4 + place[0]) * 2 + place[2], place[3]
        self.part = buf.shape[1] // pieces
        self.shared = (pieces + 1) // 2

    def plane(self, d):
        return lax.rem(self.z + d + 2 * NZ, NZ)

    def copy(self, way, s, j):
        ref = self.piece(1 - s if way == 0 else s - 1, j)
        device = {"row": self.row, "col": self.plane(1 if way == 0 else -1)}
        return remote(ref, self.send, self.recv.at[way, s % SLOTS if isinstance(s, int) else lax.rem(s, SLOTS), j], device)

    def wait(self, way, s, j):
        ref = self.piece(-s if way == 0 else s, j)
        device = {"row": self.row, "col": self.plane(1)}
        remote(ref, self.send, self.recv.at[way, s % SLOTS if isinstance(s, int) else lax.rem(s, SLOTS), j], device).wait_recv()

    def piece(self, d, j):
        return self.buf.at[self.plane(d), pl.ds(pl.multiple_of(j * self.part, 16), self.part), :]

    def step(self, s, first=False, last=False):
        @pl.loop(0, self.pieces)
        def _(j):
            for way in range(2):
                if not first:
                    self.wait(way, s - 1, j)
                if last:
                    pl.when((j < self.shared) == (way == 0))(self.copy(way, s, j).start)
                else:
                    self.copy(way, s, j).start()

    def end(self):
        @pl.loop(0, self.shared)
        def _(j):
            self.wait(0, NZ // 2, j)

        @pl.loop(self.shared, self.pieces)
        def _(j):
            self.wait(1, NZ // 2, j)


def kernel(
    x_ref, out_ref,
    slab, xrow, xcol, gram, square, grow, gcol, mrow,
    sent, sr, xr, br, gr, cr,
):
    row, z = lax.axis_index("row"), lax.axis_index("col")
    core = lax.rem(row, 2)
    x = lax.rem(row // 2, 4)
    y = row // 8
    place = (x, y, core, z)
    me = core * 16 + y * 4 + x
    up = {"row": row, "col": lax.rem(z + 1, NZ)}
    down = {"row": row, "col": lax.rem(z + NZ - 1, NZ)}

    def line(q):
        return q // 2

    def half(q):
        return pl.ds(pl.multiple_of(lax.rem(q, 2) * HALF, 16), HALF)

    gather_x = [
        PlaneGather(
            w, place, lambda i, w=w: slab.at[w, i], HALF, BLOCK, sent.at[0], sr.at[w]
        )
        for w in range(2)
    ]
    gather_c = [
        PlaneGather(
            w, place, lambda i, w=w: gcol.at[i, pl.ds(w * HALF, HALF), :], CUT, HALF, sent.at[8], cr.at[w]
        )
        for w in range(2)
    ]
    ring_x = RingGather(xrow, place, PIECES, sent.at[1], xr)
    ring_g = RingGather(grow, place, PIECES, sent.at[9], gr)
    ring_m = RingGather(mrow, place, PIECES, sent.at[10], xr)
    g0 = gather_x[0]
    east, west, north, south = g0.device(1, 0), g0.device(-1, 0), g0.device(0, 1), g0.device(0, -1)
    east2, north2 = g0.device(2, 0), g0.device(0, 2)
    sibling = g0.sibling()

    barrier = pltpu.get_barrier_semaphore()
    for device in (east, west, north, south, sibling, up, down):
        pl.semaphore_signal(barrier, inc=1, device_id=device, device_id_type=MESH)
    xrow[z] = x_ref[...].astype(jnp.bfloat16)
    slab[0, me] = x_ref[:, 0:256].astype(jnp.bfloat16)
    slab[1, me] = x_ref[:, 256:512].astype(jnp.bfloat16)
    gram[...] = jnp.zeros_like(gram)
    pl.semaphore_wait(barrier, 7)

    hands = core == line(z) // 4
    b = lax.rem(y + 4 - lax.rem(line(z), 4), 4)
    left, right = lax.rem(x + 3, 4), lax.rem(x + 1, 4)
    across = lax.rem(x + 2, 4)

    def whole(q, i):
        return xcol.at[q, i]

    def upper(q, i):
        return xcol.at[q, i, pl.ds(0, CUT), :]

    def lower(q, i):
        return xcol.at[q, i, pl.ds(CUT, HALF - CUT), :]

    def share(q, i):
        remote(whole(q, i), sent.at[7], br.at[q, 4], sibling).start()

    def spread(q, straight):
        @pl.when(straight)
        def _():
            remote(whole(q, x), sent.at[12], br.at[q, 3], east2).start()

        remote(whole(q, x), sent.at[4], br.at[q, 1], east).start()
        remote(whole(q, x), sent.at[5], br.at[q, 2], west).start()
        share(q, x)

    def source(q, straight):
        @pl.when(hands & (b == 0))
        def _():
            xcol[q, x] = xrow[q, half(z), :]

            @pl.when(straight)
            def _():
                remote(whole(q, x), sent.at[11], br.at[q, 0], north2).start()

            remote(whole(q, x), sent.at[2], br.at[q, 0], north).start()
            remote(whole(q, x), sent.at[3], br.at[q, 0], south).start()
            spread(q, straight)

    def relay(q, straight):
        @pl.when(hands & (lax.rem(b, 2) == 1))
        def _():
            remote(whole(q, x), sent.at[2], br.at[q, 0], north).wait_recv()

            @pl.when((b == 1) & jnp.logical_not(straight))
            def _():
                remote(upper(q, x), sent.at[2], br.at[q, 0], north).start()

            @pl.when((b == 3) & jnp.logical_not(straight))
            def _():
                remote(lower(q, x), sent.at[3], br.at[q, 0], south).start()

            spread(q, straight)

    def far(q, straight):
        @pl.when(hands & (b == 2))
        def _():
            remote(whole(q, x), sent.at[2], br.at[q, 0], north).wait_recv()
            spread(q, straight)

    def beside(q, straight):
        @pl.when(hands)
        def _():
            remote(whole(q, left), sent.at[4], br.at[q, 1], east).wait_recv()
            remote(whole(q, right), sent.at[5], br.at[q, 2], west).wait_recv()

            @pl.when(jnp.logical_not(straight))
            def _():
                remote(upper(q, left), sent.at[6], br.at[q, 3], east).start()
                remote(lower(q, right), sent.at[6], br.at[q, 3], west).start()

            share(q, left)
            share(q, right)

    def opposite(q, straight):
        @pl.when(hands)
        def _():
            remote(whole(q, across), sent.at[6], br.at[q, 3], east).wait_recv()
            share(q, across)

    def add(q, straight):
        @pl.when(jnp.logical_not(hands))
        def _():
            remote(xcol.at[q], sent.at[7], br.at[q, 4], sibling).wait_recv()

        gram[...] += lax.dot_general(
            xrow[q],
            xcol[q].reshape(WIDE, COLS),
            (((1,), (1,)), ((), ())),
            preferred_element_type=jnp.float32,
        )

    chain = (source, relay, far, beside, opposite, add)

    @pl.loop(0, NZ // 2 + len(chain))
    def _(t):
        @pl.when(t == 0)
        def _():
            ring_x.step(1, first=True)

        @pl.when((t > 0) & (t < 7))
        def _():
            ring_x.step(t + 1)

        @pl.when(t == 7)
        def _():
            ring_x.step(8, last=True)

        @pl.when(t == 8)
        def _():
            ring_x.end()

        for lag, action in enumerate(chain):
            n = t - lag

            both = (n > 0) & (n < 8)

            @pl.loop(0, jnp.where((n >= 0) & (n <= 8), jnp.where(both, 2, 1), 0))
            def _(side, n=n, action=action):
                action(lax.rem(z + jnp.where(side == 0, n, NZ - n), NZ), n >= STRAIGHT)

        for n, stage in enumerate(STAGES[:SLAB]):

            @pl.when(t == n)
            def _(stage=stage):
                for g in gather_x:
                    stage(g)

    gb = gram[...].astype(jnp.bfloat16)
    grow[z] = fold(gb)
    gcol[me] = gb
    square[...] = jnp.zeros_like(square)
    theirs = pl.ds((1 - core) * 16, 16)

    def unfold(ref, q):
        return jnp.concatenate([ref[q, :, 0:WIDE], ref[q, :, WIDE : 2 * WIDE]], axis=0)

    def square_step(d):
        q = lax.rem(z + d + NZ, NZ)
        square[...] += jnp.dot(
            unfold(grow, q),
            gcol[pl.ds(line(q) * 4, 4), half(q), :].reshape(WIDE, WIDE),
            preferred_element_type=jnp.float32,
        )

    ring_g.step(1, first=True)
    for s, stages in enumerate(WHEN, 1):
        if s > 1:
            ring_g.step(s)
        for n in stages:
            for g in gather_c:
                STAGES[n](g)
        if s == 2:
            for stage in STAGES[SLAB:]:
                for g in gather_x:
                    stage(g)
    ring_g.step(7)
    for w, g in enumerate(gather_c):
        g.others(gcol.at[theirs, pl.ds(w * HALF, HALF), :])

    @pl.loop(-2, 3)
    def _(d):
        square_step(d)

    ring_g.step(8, last=True)

    @pl.loop(3, 8)
    def _(d):
        square_step(d)
        square_step(-d)

    ring_g.end()
    square_step(8)

    mixed = (coef_b * gram[...] + coef_c * square[...]).astype(jnp.bfloat16)
    mrow[z] = fold(mixed)

    def product(d):
        q = lax.rem(z + d + NZ, NZ)
        left_rows = unfold(mrow, q)
        for h in range(2):
            out_ref[:, h * 256 : (h + 1) * 256] += jnp.dot(
                left_rows,
                slab[h, pl.ds(line(q) * 4, 4), half(q), :].reshape(WIDE, 256),
                preferred_element_type=jnp.float32,
            )

    ring_m.step(1, first=True)
    for g in gather_x:
        g.others(slab.at[g.way, theirs])
    out_ref[...] = coef_a * x_ref[...]
    product(0)

    @pl.loop(2, 8)
    def _(s):
        ring_m.step(s)
        product(1 - s)
        product(s - 1)

    ring_m.step(8, last=True)
    product(-7)
    product(7)
    ring_m.end()
    product(8)
    out_ref[...] = (0.2 * math.sqrt(COLS * NZ)) * out_ref[...]

    def gone(k, ref):
        remote(ref, sent.at[k], sent.at[k], up).wait_send()

    gone(0, slab.at[:, pl.ds(0, 31)])
    gone(1, xrow.at[pl.ds(0, 15)])

    @pl.when(hands)
    def _():
        @pl.when(b == 0)
        def _():
            gone(2, xcol.at[:, 0])
            gone(3, xcol.at[:, 0])
            gone(11, xcol.at[pl.ds(0, LONG), 0])

        @pl.when(b == 1)
        def _():
            gone(2, xcol.at[pl.ds(0, NZ - LONG), 0, pl.ds(0, CUT), :])

        @pl.when(b == 3)
        def _():
            gone(3, xcol.at[pl.ds(0, NZ - LONG), 0, pl.ds(CUT, HALF - CUT), :])

        gone(4, xcol.at[:, 0])
        gone(5, xcol.at[:, 0])
        gone(6, xcol.at[pl.ds(0, NZ - LONG), 0])
        gone(7, xcol)
        gone(12, xcol.at[pl.ds(0, LONG), 0])

    gone(8, gcol.at[pl.ds(0, 31)])
    gone(9, grow.at[pl.ds(0, 15)])
    gone(10, mrow.at[pl.ds(0, 15)])


def local(iterate):
    dma = pltpu.SemaphoreType.DMA
    return pl.pallas_call(
        kernel,
        out_shape=jax.ShapeDtypeStruct((BLOCK, COLS), jnp.float32),
        in_specs=[pl.BlockSpec(memory_space=pltpu.VMEM)],
        out_specs=pl.BlockSpec(memory_space=pltpu.VMEM),
        scratch_shapes=[
            pltpu.VMEM((2, 32, BLOCK, 256), jnp.bfloat16),
            pltpu.VMEM((NZ, BLOCK, COLS), jnp.bfloat16),
            pltpu.VMEM((NZ, 4, HALF, COLS), jnp.bfloat16),
            pltpu.VMEM((BLOCK, WIDE), jnp.float32),
            pltpu.VMEM((BLOCK, WIDE), jnp.float32),
            pltpu.VMEM((NZ, HALF, 2 * WIDE), jnp.bfloat16),
            pltpu.VMEM((32, BLOCK, WIDE), jnp.bfloat16),
            pltpu.VMEM((NZ, HALF, 2 * WIDE), jnp.bfloat16),
            dma((13,)),
            dma((2, 21)),
            dma((2, SLOTS, PIECES)),
            dma((NZ, 5)),
            dma((2, SLOTS, PIECES)),
            dma((2, 21)),
        ],
        compiler_params=pltpu.CompilerParams(
            collective_id=0, has_side_effects=True, vmem_limit_bytes=48 * 1024 * 1024
        ),
        cost_estimate=pl.CostEstimate(
            flops=2300000000, bytes_accessed=700000, transcendentals=0
        ),
    )(iterate)


def solution(mesh):
    return jax.shard_map(
        local,
        mesh=mesh,
        in_specs=(P("row", "col"),),
        out_specs=P("row", "col"),
        check_vma=False,
    )
```
